256 devices in a mesh: box: 64 (over x, z, y_hi), rhs: 4 (over y_lo, core).
Axes of the slice: x: 4, y: 4 (y_hi: 2, y_lo: 2; y = y_hi * 2 + y_lo), z: 8, core: 2. Of those that a mesh axis runs over, the one named last changes fastest.
Arguments:
- rhs_block: float32 [256, 256, 512], P('box', 'rhs'), may hold values from -6 to 6
- near_blocks: float32 [256, 3, 256, 512], P('box'), may hold values from -0.15625 to 0.15625
- near_mask: int32 [2, 256], P(None, 'box'), may hold values 0 or 1
- compress: float32 [256, 256, 128], P('box'), may hold values from -0.25 to 0.25
- butterfly: float32 [8, 256, 2, 64, 128], P(None, 'box'), may hold values from -0.375 to 0.375
- expand: float32 [256, 64, 512], P('box'), may hold values from -0.5 to 0.5
Outputs:
- field: float32 [256, 256, 512], P('box', 'rhs')
The draws below stay inside these ranges and needn't reach their ends.
All inputs are finite; a program needn't handle non-finite values. No bound on the sum of `near_mask` on one device may be relied on, other than what follows from the above.
Results may differ from the reference program's by a relative error of at most 0.0001.
Values sent between devices are 32-bit elements; how exact they have to be, the bound alone decides.
No kernel may reach another device: no remote copies, remote signals or barrier semaphores. Data moves between devices by JAX's collectives and lax.ppermute only.
A program may use at most 64 MiB of HBM per device.

```python
import jax
import jax.numpy as jnp
from jax import lax

LEAF = 256
RANK = 64
NBOX = 256
RHS = 256
LEVELS = 8


def set_ends(values, stream_key, smallest, largest):
    longest = values.shape.index(max(values.shape))
    spots = []
    for shift in (0, 1):
        where = [jax.random.randint(jax.random.fold_in(stream_key, axis), (), 0, length) for axis, length in enumerate(values.shape)]
        where[longest] = (where[longest] + shift) % values.shape[longest]
        spots.append(tuple(where))
    return values.at[spots[0]].set(smallest).at[spots[1]].set(largest)


def block_levels(rng, dims, cuts, least, largest):
    factor_of, own = 1.0, jax.random.fold_in(rng, 6)
    for position, parts in cuts:
        steps = jnp.exp(jax.random.uniform(jax.random.fold_in(own, position), (parts,), jnp.float32, least / len(cuts), largest / len(cuts)))
        factor_of = factor_of * jnp.repeat(steps, dims[position] // parts).reshape([-1 if axis == position else 1 for axis in range(len(dims))])
    return factor_of


def noise(rng, dims, scale, bound, split=(), kind=jnp.bfloat16):
    array = scale * jax.random.normal(rng, dims, jnp.float32)
    if split:
        array = array * block_levels(rng, dims, split, -0.22, 0.18)
    return jnp.clip(array, -bound, bound).astype(kind)


def setup_inputs(seed: int = 0) -> dict:
    seeds = jax.random.split(jax.random.key(seed), 7)
    return {
        "rhs_block": noise(seeds[0], (NBOX, RHS, 2 * LEAF), 1.0, 6.0, ((0, 64), (1, 4)), jnp.float32),
        "near_blocks": noise(seeds[1], (NBOX, 3, LEAF, 2 * LEAF), (6 * LEAF) ** -0.5, 0.15625, ((0, 64),), jnp.float32),
        "near_mask": set_ends((jax.random.randint(seeds[2], (2, NBOX), 0, 4) < 3).astype(jnp.int32), jax.random.fold_in(seeds[2], 1), 0, 1),
        "compress": noise(seeds[3], (NBOX, LEAF, 2 * RANK), (2 * LEAF) ** -0.5, 0.25, ((0, 64),), jnp.float32),
        "butterfly": noise(seeds[4], (LEVELS, NBOX, 2, RANK, 2 * RANK), (4 * RANK) ** -0.5, 0.375, ((1, 64),), jnp.float32),
        "expand": noise(seeds[5], (NBOX, RANK, 2 * LEAF), (2 * RANK) ** -0.5, 0.5, ((0, 64),), jnp.float32),
    }


def complex_apply(values, weights):
    half = values.shape[-1] // 2
    width = weights.shape[-1] // 2
    real_in = jnp.einsum("bri,bio->bro", values[..., :half], weights, precision=lax.Precision.HIGHEST)
    imag_in = jnp.einsum("bri,bio->bro", values[..., half:], weights, precision=lax.Precision.HIGHEST)
    real_out = real_in[..., :width] - imag_in[..., width:]
    imag_out = real_in[..., width:] + imag_in[..., :width]
    return jnp.concatenate([real_out, imag_out], axis=-1)


def partner_boxes(coef, level):
    half = 2 ** level
    shaped = coef.reshape(coef.shape[0] // (2 * half), 2, half, coef.shape[1], coef.shape[2])
    return jnp.flip(shaped, 1).reshape(coef.shape)


def reference(rhs_block, near_blocks, near_mask, compress, butterfly, expand):
    masks = near_mask.astype(jnp.float32)
    before = complex_apply(jnp.roll(rhs_block, 1, axis=0), near_blocks[:, 0])
    middle = complex_apply(rhs_block, near_blocks[:, 1])
    after = complex_apply(jnp.roll(rhs_block, -1, axis=0), near_blocks[:, 2])
    near = before * masks[0][:, None, None] + middle + after * masks[1][:, None, None]
    coef = complex_apply(rhs_block, compress)
    for level in range(LEVELS):
        weights = butterfly[level]
        other = partner_boxes(coef, level)
        coef = complex_apply(coef, weights[:, 0]) + complex_apply(other, weights[:, 1])
    far = complex_apply(coef, expand)
    return near + far
```

```python
import jax
import jax.numpy as jnp
from jax import lax
from jax.sharding import PartitionSpec as P


def product(values, weights):
    return jnp.einsum("bri,bio->bro", values, weights, precision=lax.Precision.HIGH)


def turned(values):
    half = values.shape[-1] // 2
    return jnp.concatenate([-values[..., half:], values[..., :half]], axis=-1)


def expanded(weights):
    return jnp.concatenate([weights, turned(weights)], axis=-2)


def level_weights(weights):
    count, _, rank, width = weights.shape
    return expanded(weights).reshape(count, 4 * rank, width)


def stacked(values):
    half = values.shape[-1] // 2
    return jnp.concatenate([values[..., :half], values[..., half:]], axis=1)


def unstacked(values):
    half = values.shape[1] // 2
    return values[:, :half] + turned(values[:, half:])


def local_partner(coef, level):
    half = 2**level
    shaped = coef.reshape(coef.shape[0] // (2 * half), 2, half, coef.shape[1], coef.shape[2])
    return jnp.flip(shaped, 1).reshape(coef.shape)


def exchange(value, mask):
    pairs = [(source, source ^ mask) for source in range(lax.axis_size("box"))]
    return lax.ppermute(value, "box", pairs)


def on_device(rhs_block, near_blocks, near_mask, compress, butterfly, expand):
    count = rhs_block.shape[0]
    local_bits = count.bit_length() - 1
    levels = butterfly.shape[0]
    size = lax.axis_size("box")

    coef = product(rhs_block, expanded(compress))
    for level in range(local_bits):
        other = local_partner(coef, level)
        coef = product(jnp.concatenate([coef, other], -1), level_weights(butterfly[level]))

    forward = [(i, (i + 1) % size) for i in range(size)]
    backward = [(target, source) for source, target in forward]
    masks = near_mask.astype(jnp.float32)
    low = lax.ppermute(rhs_block[count - 1 :], "box", forward)
    high = lax.ppermute(rhs_block[:1], "box", backward)
    before = jnp.concatenate([low, rhs_block[:-1]], 0) * masks[0][:, None, None]
    after = jnp.concatenate([rhs_block[1:], high], 0) * masks[1][:, None, None]

    near = product(stacked(rhs_block), near_blocks[:, 1])
    near = near + product(stacked(before), near_blocks[:, 0])
    near = near + product(stacked(after), near_blocks[:, 2])
    near = unstacked(near)

    for level in range(local_bits, levels):
        other = exchange(coef, 2 ** (level - local_bits))
        coef = product(jnp.concatenate([coef, other], -1), level_weights(butterfly[level]))
    return near + product(coef, expanded(expand))


def solution(mesh):
    placed = (
        P("box", "rhs", None),
        P("box", None, None, None),
        P(None, "box"),
        P("box", None, None),
        P(None, "box", None, None, None),
        P("box", None, None),
    )
    return jax.shard_map(
        on_device, mesh=mesh, in_specs=placed, out_specs=P("box", "rhs", None), check_vma=False
    )
```

```python
import jax
import jax.numpy as jnp
from jax import lax
from jax.experimental import pallas as pl
from jax.experimental.pallas import tpu as pltpu
from jax.sharding import PartitionSpec as P

VMEM = pl.BlockSpec(memory_space=pltpu.VMEM)
ANY = pl.BlockSpec(memory_space=pl.ANY)
SMALL = pltpu.CompilerParams(vmem_limit_bytes=8 << 20)
F32 = jnp.float32
BF16 = jnp.bfloat16


def in_vmem(value):
    return pltpu.with_memory_space_constraint(value, pltpu.VMEM)


def cost(us):
    return pl.CostEstimate(flops=int(us * 1e8), bytes_accessed=int(us * 1e6), transcendentals=0)


def turned(values):
    half = values.shape[-1] // 2
    return jnp.concatenate([-values[..., half:], values[..., :half]], axis=-1)


def split(value):
    high = value.astype(BF16)
    return high, (value - high.astype(F32)).astype(BF16)


def dot(left, right):
    return jnp.dot(left, right, preferred_element_type=F32)


def apply_split(values, high, low):
    rows = values.shape[0]
    first, second = split(values)
    both = dot(jnp.concatenate([first, second], axis=0), high)
    return both[:rows] + (both[rows:] + dot(first, low))


def complex_dot(values, weights):
    half = values.shape[-1] // 2
    rows = jnp.concatenate([values[:, :half], values[:, half:]], axis=0)
    high, low = split(weights)
    both = apply_split(rows, high, low)
    count = values.shape[0]
    return both[:count] + turned(both[count:])


def level_dot(own, other, weights):
    half = own.shape[-1] // 2
    real = jnp.concatenate([own[:, :half], other[:, :half]], axis=1)
    imag = jnp.concatenate([own[:, half:], other[:, half:]], axis=1)
    high, low = split(weights.reshape(2 * half, weights.shape[-1]))
    count = own.shape[0]
    both = apply_split(jnp.concatenate([real, imag], axis=0), high, low)
    return both[:count] + turned(both[count:])


def head_kernel(x_hbm, c_hbm, w_hbm, out, x_buf, c_buf, w_buf, sems):
    count = x_buf.shape[0]
    copies = []
    for b in range(count):
        copies.append(pltpu.make_async_copy(x_hbm.at[b], x_buf.at[b], sems.at[2 * b]))
        copies.append(pltpu.make_async_copy(c_hbm.at[b], c_buf.at[b], sems.at[2 * b + 1]))
    levels = w_buf.shape[0]
    last = [
        pltpu.make_async_copy(w_hbm.at[level], w_buf.at[level], sems.at[2 * count + level])
        for level in range(levels)
    ]
    for copy in copies + last:
        copy.start()
    coef = []
    for b in range(count):
        copies[2 * b].wait()
        copies[2 * b + 1].wait()
        coef.append(complex_dot(x_buf[b], c_buf[b]))
    for level in range(levels):
        last[level].wait()
        coef = [level_dot(coef[b], coef[b ^ (1 << level)], w_buf[level, b]) for b in range(count)]
    for b in range(count):
        out[b] = coef[b]


def head(x, compress, butterfly, levels):
    count, rows, _ = x.shape
    width = compress.shape[-1]
    return pl.pallas_call(
        head_kernel,
        out_shape=[pltpu.VMEM((count, rows, width), F32), pltpu.VMEM(x.shape, F32)],
        in_specs=[ANY, ANY, ANY],
        out_specs=[VMEM, VMEM],
        scratch_shapes=[
            pltpu.VMEM(compress.shape, F32),
            pltpu.VMEM((levels,) + butterfly.shape[1:], F32),
            pltpu.SemaphoreType.DMA((2 * count + levels,)),
        ],
        cost_estimate=cost(2.5),
        name="head",
    )(x, compress, butterfly)


def prepare_kernel(level, weights_ref, after, high, low):
    del after
    _, count, slots, rank, _ = weights_ref.shape
    for b in range(count):
        for s in range(slots):
            base = 2 * rank * s
            weights = weights_ref[level, b, s]
            high[b, base : base + rank], low[b, base : base + rank] = split(weights)
            base += rank
            high[b, base : base + rank], low[b, base : base + rank] = split(turned(weights))


def prepare(level, butterfly, after):
    _, count, slots, rank, width = butterfly.shape
    shape = pltpu.VMEM((count, 2 * slots * rank, width), BF16)
    return pl.pallas_call(
        lambda *refs: prepare_kernel(level, *refs),
        out_shape=[shape, shape],
        in_specs=[VMEM, VMEM],
        out_specs=[VMEM, VMEM],
        compiler_params=SMALL,
        cost_estimate=cost(0.25),
        name=f"prepare{level}",
    )(in_vmem(butterfly), in_vmem(after))


def prepare_expand_kernel(weights_ref, after, high, low):
    del after
    count, rank, _ = weights_ref.shape
    for b in range(count):
        weights = weights_ref[b]
        high[b, :rank], low[b, :rank] = split(weights)
        high[b, rank:], low[b, rank:] = split(turned(weights))


def prepare_expand(expand, after):
    count, rank, width = expand.shape
    shape = pltpu.VMEM((count, 2 * rank, width), BF16)
    return pl.pallas_call(
        prepare_expand_kernel,
        out_shape=[shape, shape],
        in_specs=[VMEM, VMEM],
        out_specs=[VMEM, VMEM],
        compiler_params=SMALL,
        cost_estimate=cost(0.25),
        name="prepare_expand",
    )(in_vmem(expand), in_vmem(after))


def level_kernel(own, other, high, low, *rest):
    out = rest[-1]
    for b in range(own.shape[0]):
        out[b] = apply_split(jnp.concatenate([own[b], other[b]], axis=1), high[b], low[b])


def level_step(own, other, high, low, name, *ties):
    values = (own, other, high, low) + ties
    return pl.pallas_call(
        level_kernel,
        out_shape=pltpu.VMEM(own.shape, F32),
        in_specs=[VMEM] * len(values),
        out_specs=VMEM,
        compiler_params=SMALL,
        cost_estimate=cost(0.25),
        name=name,
    )(*map(in_vmem, values))


def last_kernel(own, other, high, low, e_high, e_low, near, out_hbm, out_buf, sems):
    copies = []
    for b in range(own.shape[0]):
        coef = apply_split(jnp.concatenate([own[b], other[b]], axis=1), high[b], low[b])
        out_buf[b] = near[b] + apply_split(coef, e_high[b], e_low[b])
        copies.append(pltpu.make_async_copy(out_buf.at[b], out_hbm.at[b], sems.at[b]))
        copies[b].start()
    for copy in copies:
        copy.wait()


def last_step(own, other, high, low, e_high, e_low, near):
    return pl.pallas_call(
        last_kernel,
        out_shape=jax.ShapeDtypeStruct(near.shape, F32),
        in_specs=[VMEM] * 7,
        out_specs=ANY,
        scratch_shapes=[
            pltpu.VMEM(near.shape, F32),
            pltpu.SemaphoreType.DMA((near.shape[0],)),
        ],
        compiler_params=SMALL,
        cost_estimate=cost(1.0),
        name="last",
    )(*map(in_vmem, (own, other, high, low, e_high, e_low, near)))


def product(values, weights):
    return jnp.einsum("bri,bio->bro", values, weights, precision=lax.Precision.HIGH)


def stacked(values):
    half = values.shape[-1] // 2
    return jnp.concatenate([values[..., :half], values[..., half:]], axis=1)


def unstacked(values):
    half = values.shape[1] // 2
    return values[:, :half] + turned(values[:, half:])


def exchange(value, mask):
    pairs = [(source, source ^ mask) for source in range(lax.axis_size("box"))]
    return lax.ppermute(value, "box", pairs)


def after(value, other):
    return lax.optimization_barrier((value, other))[0]


def on_device(rhs_block, near_blocks, near_mask, compress, butterfly, expand):
    count = rhs_block.shape[0]
    local_bits = count.bit_length() - 1
    size = lax.axis_size("box")
    even = lax.axis_index("box") % 2 == 0
    masks = near_mask.astype(F32)

    def weights(level, coef):
        return prepare(level, butterfly, coef)

    coef, x = head(rhs_block, compress, butterfly, local_bits)
    first, final = x[:1], x[count - 1 :]
    pairs = [(i, (i - 1 if i % 2 == 0 else i + 1) % size) for i in range(size)]

    other = exchange(coef, 1)
    level2 = weights(2, coef)
    inner = exchange(after(jnp.where(even, final, first), level2[0]), 1)
    coef = level_step(coef, other, *level2, "level2")

    other = exchange(coef, 2)
    level3 = weights(3, coef)
    coef = level_step(coef, other, *level3, "level3", inner)

    other = exchange(coef, 4)
    level4 = weights(4, coef)
    near = product(stacked(after(x, level4[0])), near_blocks[:, 1])
    level5 = weights(5, coef)
    level6 = weights(6, coef)
    level7 = weights(7, coef)
    coef = level_step(coef, other, *level4, "level4", *level5, *level6, *level7, near)

    other = exchange(coef, 8)
    far = prepare_expand(expand, coef)
    outer = lax.ppermute(after(jnp.where(even, first, final), far[0]), "box", pairs)
    coef = level_step(coef, other, *level5, "level5")

    other = exchange(coef, 16)
    coef = level_step(coef, other, *level6, "level6")

    other = exchange(coef, 32)
    below = jnp.where(even, outer, inner)
    above = jnp.where(even, inner, outer)
    below, above, _ = lax.optimization_barrier((below, above, coef))
    before = jnp.concatenate([below, x[:-1]], 0) * masks[0][:, None, None]
    behind = jnp.concatenate([x[1:], above], 0) * masks[1][:, None, None]
    near = near + product(stacked(before), near_blocks[:, 0])
    near = near + product(stacked(behind), near_blocks[:, 2])
    return last_step(coef, other, *level7, *far, unstacked(near))


def solution(mesh):
    placed = (
        P("box", "rhs", None),
        P("box", None, None, None),
        P(None, "box"),
        P("box", None, None),
        P(None, "box", None, None, None),
        P("box", None, None),
    )
    return jax.shard_map(
        on_device, mesh=mesh, in_specs=placed, out_specs=P("box", "rhs", None), check_vma=False
    )
```

```python
import jax
import jax.numpy as jnp
from jax import lax
from jax.experimental import pallas as pl
from jax.experimental.pallas import tpu as pltpu
from jax.sharding import PartitionSpec as P

VMEM = pl.BlockSpec(memory_space=pltpu.VMEM)
ANY = pl.BlockSpec(memory_space=pl.ANY)
SMALL = pltpu.CompilerParams(vmem_limit_bytes=8 << 20)
F32 = jnp.float32
BF16 = jnp.bfloat16


def in_vmem(value):
    return pltpu.with_memory_space_constraint(value, pltpu.VMEM)


def cost(us):
    return pl.CostEstimate(flops=int(us * 1e8), bytes_accessed=int(us * 1e6), transcendentals=0)


def turned(values):
    half = values.shape[-1] // 2
    return jnp.concatenate([-values[..., half:], values[..., :half]], axis=-1)


def split(value):
    high = value.astype(BF16)
    return high, (value - high.astype(F32)).astype(BF16)


def dot(left, right):
    return jnp.dot(left, right, preferred_element_type=F32)


def apply_split(values, high, low):
    rows = values.shape[0]
    first, second = split(values)
    both = dot(jnp.concatenate([first, second], axis=0), high)
    return both[:rows] + (both[rows:] + dot(first, low))


def complex_dot(values, weights):
    half = values.shape[-1] // 2
    rows = jnp.concatenate([values[:, :half], values[:, half:]], axis=0)
    high, low = split(weights)
    both = apply_split(rows, high, low)
    count = values.shape[0]
    return both[:count] + turned(both[count:])


def level_dot(own, other, weights):
    half = own.shape[-1] // 2
    real = jnp.concatenate([own[:, :half], other[:, :half]], axis=1)
    imag = jnp.concatenate([own[:, half:], other[:, half:]], axis=1)
    high, low = split(weights.reshape(2 * half, weights.shape[-1]))
    count = own.shape[0]
    both = apply_split(jnp.concatenate([real, imag], axis=0), high, low)
    return both[:count] + turned(both[count:])


def head_kernel(x_hbm, c_hbm, w_hbm, out, x_buf, c_buf, w_buf, sems):
    count = x_buf.shape[0]
    copies = []
    for b in range(count):
        copies.append(pltpu.make_async_copy(x_hbm.at[b], x_buf.at[b], sems.at[2 * b]))
        copies.append(pltpu.make_async_copy(c_hbm.at[b], c_buf.at[b], sems.at[2 * b + 1]))
    levels = w_buf.shape[0]
    last = [
        pltpu.make_async_copy(w_hbm.at[level], w_buf.at[level], sems.at[2 * count + level])
        for level in range(levels)
    ]
    for copy in copies + last:
        copy.start()
    coef = []
    for b in range(count):
        copies[2 * b].wait()
        copies[2 * b + 1].wait()
        coef.append(complex_dot(x_buf[b], c_buf[b]))
    for level in range(levels):
        last[level].wait()
        coef = [level_dot(coef[b], coef[b ^ (1 << level)], w_buf[level, b]) for b in range(count)]
    for b in range(count):
        out[b] = coef[b]


def head(x, compress, butterfly, levels):
    count, rows, _ = x.shape
    width = compress.shape[-1]
    return pl.pallas_call(
        head_kernel,
        out_shape=[pltpu.VMEM((count, rows, width), F32), pltpu.VMEM(x.shape, F32)],
        in_specs=[ANY, ANY, ANY],
        out_specs=[VMEM, VMEM],
        scratch_shapes=[
            pltpu.VMEM(compress.shape, F32),
            pltpu.VMEM((levels,) + butterfly.shape[1:], F32),
            pltpu.SemaphoreType.DMA((2 * count + levels,)),
        ],
        cost_estimate=cost(2.5),
        name="head",
    )(x, compress, butterfly)


def prepare_kernel(level, weights_ref, after, high, low):
    del after
    _, count, slots, rank, _ = weights_ref.shape
    for b in range(count):
        for s in range(slots):
            base = 2 * rank * s
            weights = weights_ref[level, b, s]
            high[b, base : base + rank], low[b, base : base + rank] = split(weights)
            base += rank
            high[b, base : base + rank], low[b, base : base + rank] = split(turned(weights))


def prepare(level, butterfly, after):
    _, count, slots, rank, width = butterfly.shape
    shape = pltpu.VMEM((count, 2 * slots * rank, width), BF16)
    return pl.pallas_call(
        lambda *refs: prepare_kernel(level, *refs),
        out_shape=[shape, shape],
        in_specs=[VMEM, VMEM],
        out_specs=[VMEM, VMEM],
        compiler_params=SMALL,
        cost_estimate=cost(0.25),
        name=f"prepare{level}",
    )(in_vmem(butterfly), in_vmem(after))


def store_expanded(high, low, where, weights):
    rank = weights.shape[0]
    high[(*where, slice(0, rank))], low[(*where, slice(0, rank))] = split(weights)
    weights = turned(weights)
    high[(*where, slice(rank, None))], low[(*where, slice(rank, None))] = split(weights)


def fuse_last_kernel(weights_ref, expand_ref, after, high, low):
    del after
    level = weights_ref.shape[0] - 1
    _, count, slots, rank, width = weights_ref.shape
    for b in range(count):
        expand = expand_ref[b]
        expand = jnp.concatenate([expand, turned(expand)], axis=0)
        both = apply_split(weights_ref[level, b].reshape(slots * rank, width), *split(expand))
        for s in range(slots):
            store_expanded(high, low, (b, s), both[s * rank : (s + 1) * rank])


def fuse_last(butterfly, expand, after):
    _, count, slots, rank, width = butterfly.shape
    shape = pltpu.VMEM((count, slots, width, expand.shape[-1]), BF16)
    return pl.pallas_call(
        fuse_last_kernel,
        out_shape=[shape, shape],
        in_specs=[VMEM] * 3,
        out_specs=[VMEM] * 2,
        compiler_params=SMALL,
        cost_estimate=cost(1.0),
        name="fuse_last",
    )(*map(in_vmem, (butterfly, expand, after)))


def fuse_two_kernel(weights_ref, fetched_ref, m_high, m_low, after, high, low):
    del after
    level = weights_ref.shape[0] - 2
    _, count, slots, rank, width = weights_ref.shape
    for b in range(count):
        for half, weights in enumerate((weights_ref[level, b], fetched_ref[0, b])):
            rows = weights.reshape(slots * rank, width)
            both = apply_split(rows, m_high[b, half], m_low[b, half])
            for s in range(slots):
                store_expanded(high, low, (b, 2 * half + s), both[s * rank : (s + 1) * rank])


def fuse_two(butterfly, fetched, m_high, m_low, after):
    count, slots, width, out = m_high.shape
    shape = pltpu.VMEM((count, 2 * slots, width, out), BF16)
    return pl.pallas_call(
        fuse_two_kernel,
        out_shape=[shape, shape],
        in_specs=[VMEM] * 5,
        out_specs=[VMEM] * 2,
        compiler_params=SMALL,
        cost_estimate=cost(1.5),
        name="fuse_two",
    )(*map(in_vmem, (butterfly, fetched, m_high, m_low, after)))


def add_part_kernel(slot, near, coef, high, low, out):
    for b in range(near.shape[0]):
        out[b] = near[b] + apply_split(coef[b], high[b, slot], low[b, slot])


def add_part(slot, *values):
    return pl.pallas_call(
        lambda *refs: add_part_kernel(slot, *refs),
        out_shape=pltpu.VMEM(values[0].shape, F32),
        in_specs=[VMEM] * 4,
        out_specs=VMEM,
        compiler_params=SMALL,
        cost_estimate=cost(0.5),
        name=f"part{slot}",
    )(*map(in_vmem, values))


def level_kernel(own, other, high, low, *rest):
    out = rest[-1]
    for b in range(own.shape[0]):
        out[b] = apply_split(jnp.concatenate([own[b], other[b]], axis=1), high[b], low[b])


def level_step(own, other, high, low, name, *ties):
    values = (own, other, high, low) + ties
    return pl.pallas_call(
        level_kernel,
        out_shape=pltpu.VMEM(own.shape, F32),
        in_specs=[VMEM] * len(values),
        out_specs=VMEM,
        compiler_params=SMALL,
        cost_estimate=cost(0.25),
        name=name,
    )(*map(in_vmem, values))


def last_kernel(two, both, high, low, near, out_hbm, out_buf, sems):
    count = two.shape[0]
    rows = 2 * high.shape[2]
    copies = []
    for b in range(count):
        coef = jnp.concatenate([two[b], both[b]], axis=1)
        weights = (part[b, 2:].reshape(rows, part.shape[-1]) for part in (high, low))
        out_buf[b] = near[b] + apply_split(coef, *weights)
        copies.append(pltpu.make_async_copy(out_buf.at[b], out_hbm.at[b], sems.at[b]))
        copies[b].start()
    for copy in copies:
        copy.wait()


def last_step(*values):
    near = values[-1]
    return pl.pallas_call(
        last_kernel,
        out_shape=jax.ShapeDtypeStruct(near.shape, F32),
        in_specs=[VMEM] * len(values),
        out_specs=ANY,
        scratch_shapes=[
            pltpu.VMEM(near.shape, F32),
            pltpu.SemaphoreType.DMA((near.shape[0],)),
        ],
        compiler_params=SMALL,
        cost_estimate=cost(1.0),
        name="last",
    )(*map(in_vmem, values))


def product(values, weights):
    return jnp.einsum("bri,bio->bro", values, weights, precision=lax.Precision.HIGH)


def stacked(values):
    half = values.shape[-1] // 2
    return jnp.concatenate([values[..., :half], values[..., half:]], axis=1)


def unstacked(values):
    half = values.shape[1] // 2
    return values[:, :half] + turned(values[:, half:])


def exchange(value, mask):
    pairs = [(source, source ^ mask) for source in range(lax.axis_size("box"))]
    return lax.ppermute(value, "box", pairs)


def after(value, other):
    return lax.optimization_barrier((value, other))[0]


def on_device(rhs_block, near_blocks, near_mask, compress, butterfly, expand):
    count = rhs_block.shape[0]
    local_bits = count.bit_length() - 1
    size = lax.axis_size("box")
    even = lax.axis_index("box") % 2 == 0
    masks = near_mask.astype(F32)

    def weights(level, coef):
        return prepare(level, butterfly, coef)

    coef, x = head(rhs_block, compress, butterfly, local_bits)
    first, final = x[:1], x[count - 1 :]
    pairs = [(i, (i - 1 if i % 2 == 0 else i + 1) % size) for i in range(size)]

    other = exchange(coef, 1)
    level2 = weights(2, coef)
    coef = level_step(coef, other, *level2, "level2")

    other = exchange(coef, 2)
    level3 = weights(3, coef)
    inner = exchange(after(jnp.where(even, final, first), level3[0]), 1)
    coef = level_step(coef, other, *level3, "level3")

    other = exchange(coef, 4)
    level4 = weights(4, coef)
    fetched = exchange(after(butterfly[6:7], level4[0]), 32)
    near = product(stacked(after(x, level4[0])), near_blocks[:, 1])
    level5 = weights(5, coef)
    last = fuse_last(butterfly, expand, level4[0])
    coef = level_step(coef, other, *level4, "level4", *level5, *last, near, inner)

    other = exchange(coef, 8)
    fused = fuse_two(butterfly, fetched, *last, coef)
    outer = lax.ppermute(after(jnp.where(even, first, final), fused[0]), "box", pairs)
    coef = level_step(coef, other, *level5, "level5", *fused)

    two = exchange(coef, 32)
    both = exchange(coef, 48)
    one = exchange(coef, 16)
    below = jnp.where(even, outer, inner)
    above = jnp.where(even, inner, outer)
    below, above, _ = lax.optimization_barrier((below, above, coef))
    before = jnp.concatenate([below, x[:-1]], 0) * masks[0][:, None, None]
    behind = jnp.concatenate([x[1:], above], 0) * masks[1][:, None, None]
    near = near + product(stacked(before), near_blocks[:, 0])
    near = unstacked(near + product(stacked(behind), near_blocks[:, 2]))
    near = add_part(0, near, coef, *fused)
    near = add_part(1, near, one, *fused)
    return last_step(two, both, *fused, near)


def solution(mesh):
    placed = (
        P("box", "rhs", None),
        P("box", None, None, None),
        P(None, "box"),
        P("box", None, None),
        P(None, "box", None, None, None),
        P("box", None, None),
    )
    return jax.shard_map(
        on_device, mesh=mesh, in_specs=placed, out_specs=P("box", "rhs", None), check_vma=False
    )
```

```python
import jax
import jax.numpy as jnp
from jax import lax
from jax.experimental import pallas as pl
from jax.experimental.pallas import tpu as pltpu
from jax.sharding import PartitionSpec as P

VMEM = pl.BlockSpec(memory_space=pltpu.VMEM)
ANY = pl.BlockSpec(memory_space=pl.ANY)
SMALL = pltpu.CompilerParams(vmem_limit_bytes=8 << 20)
F32 = jnp.float32
BF16 = jnp.bfloat16


def in_vmem(value):
    return pltpu.with_memory_space_constraint(value, pltpu.VMEM)


def cost(us):
    return pl.CostEstimate(flops=int(us * 1e8), bytes_accessed=int(us * 1e6), transcendentals=0)


def turned(values):
    half = values.shape[-1] // 2
    return jnp.concatenate([-values[..., half:], values[..., :half]], axis=-1)


def split(value):
    high = value.astype(BF16)
    return high, (value - high.astype(F32)).astype(BF16)


def dot(left, right):
    return jnp.dot(left, right, preferred_element_type=F32)


def apply_split(values, high, low):
    rows = values.shape[0]
    first, second = split(values)
    both = dot(jnp.concatenate([first, second], axis=0), high)
    return both[:rows] + (both[rows:] + dot(first, low))


def complex_dot(values, weights):
    half = values.shape[-1] // 2
    rows = jnp.concatenate([values[:, :half], values[:, half:]], axis=0)
    high, low = split(weights)
    both = apply_split(rows, high, low)
    count = values.shape[0]
    return both[:count] + turned(both[count:])


def level_dot(own, other, weights):
    half = own.shape[-1] // 2
    real = jnp.concatenate([own[:, :half], other[:, :half]], axis=1)
    imag = jnp.concatenate([own[:, half:], other[:, half:]], axis=1)
    high, low = split(weights.reshape(2 * half, weights.shape[-1]))
    count = own.shape[0]
    both = apply_split(jnp.concatenate([real, imag], axis=0), high, low)
    return both[:count] + turned(both[count:])


def head_kernel(x_hbm, c_hbm, w_hbm, out, x_buf, c_buf, w_buf, sems):
    count = x_buf.shape[0]
    copies = []
    for b in range(count):
        copies.append(pltpu.make_async_copy(x_hbm.at[b], x_buf.at[b], sems.at[2 * b]))
        copies.append(pltpu.make_async_copy(c_hbm.at[b], c_buf.at[b], sems.at[2 * b + 1]))
    levels = w_buf.shape[0]
    last = [
        pltpu.make_async_copy(w_hbm.at[level], w_buf.at[level], sems.at[2 * count + level])
        for level in range(levels)
    ]
    for copy in copies + last:
        copy.start()
    coef = []
    for b in range(count):
        copies[2 * b].wait()
        copies[2 * b + 1].wait()
        coef.append(complex_dot(x_buf[b], c_buf[b]))
    for level in range(levels):
        last[level].wait()
        coef = [level_dot(coef[b], coef[b ^ (1 << level)], w_buf[level, b]) for b in range(count)]
    for b in range(count):
        out[b] = coef[b]


def head(x, compress, butterfly, levels):
    count, rows, _ = x.shape
    width = compress.shape[-1]
    return pl.pallas_call(
        head_kernel,
        out_shape=[pltpu.VMEM((count, rows, width), F32), pltpu.VMEM(x.shape, F32)],
        in_specs=[ANY, ANY, ANY],
        out_specs=[VMEM, VMEM],
        scratch_shapes=[
            pltpu.VMEM(compress.shape, F32),
            pltpu.VMEM((levels,) + butterfly.shape[1:], F32),
            pltpu.SemaphoreType.DMA((2 * count + levels,)),
        ],
        cost_estimate=cost(2.5),
        name="head",
    )(x, compress, butterfly)


def prepare_kernel(level, weights_ref, after, high, low):
    del after
    _, count, slots, rank, _ = weights_ref.shape
    for b in range(count):
        for s in range(slots):
            base = 2 * rank * s
            weights = weights_ref[level, b, s]
            high[b, base : base + rank], low[b, base : base + rank] = split(weights)
            base += rank
            high[b, base : base + rank], low[b, base : base + rank] = split(turned(weights))


def prepare(level, butterfly, after):
    _, count, slots, rank, width = butterfly.shape
    shape = pltpu.VMEM((count, 2 * slots * rank, width), BF16)
    return pl.pallas_call(
        lambda *refs: prepare_kernel(level, *refs),
        out_shape=[shape, shape],
        in_specs=[VMEM, VMEM],
        out_specs=[VMEM, VMEM],
        compiler_params=SMALL,
        cost_estimate=cost(0.25),
        name=f"prepare{level}",
    )(in_vmem(butterfly), in_vmem(after))


def store_expanded(high, low, where, weights):
    rank = weights.shape[0]
    high[(*where, slice(0, rank))], low[(*where, slice(0, rank))] = split(weights)
    weights = turned(weights)
    high[(*where, slice(rank, None))], low[(*where, slice(rank, None))] = split(weights)


def fuse_last_kernel(weights_ref, expand_ref, after, high, low):
    del after
    level = weights_ref.shape[0] - 1
    _, count, slots, rank, width = weights_ref.shape
    for b in range(count):
        expand = expand_ref[b]
        expand = jnp.concatenate([expand, turned(expand)], axis=0)
        both = apply_split(weights_ref[level, b].reshape(slots * rank, width), *split(expand))
        for s in range(slots):
            store_expanded(high, low, (b, s), both[s * rank : (s + 1) * rank])


def fuse_last(butterfly, expand, after):
    _, count, slots, rank, width = butterfly.shape
    shape = pltpu.VMEM((count, slots, width, expand.shape[-1]), BF16)
    return pl.pallas_call(
        fuse_last_kernel,
        out_shape=[shape, shape],
        in_specs=[VMEM] * 3,
        out_specs=[VMEM] * 2,
        compiler_params=SMALL,
        cost_estimate=cost(1.0),
        name="fuse_last",
    )(*map(in_vmem, (butterfly, expand, after)))


def fuse_two_kernel(weights_ref, fetched_ref, m_high, m_low, after, high, low):
    del after
    level = weights_ref.shape[0] - 2
    _, count, slots, rank, width = weights_ref.shape
    for b in range(count):
        for half, weights in enumerate((weights_ref[level, b], fetched_ref[0, b])):
            rows = weights.reshape(slots * rank, width)
            both = apply_split(rows, m_high[b, half], m_low[b, half])
            for s in range(slots):
                store_expanded(high, low, (b, 2 * half + s), both[s * rank : (s + 1) * rank])


def fuse_two(butterfly, fetched, m_high, m_low, after):
    count, slots, width, out = m_high.shape
    shape = pltpu.VMEM((count, 2 * slots, width, out), BF16)
    return pl.pallas_call(
        fuse_two_kernel,
        out_shape=[shape, shape],
        in_specs=[VMEM] * 5,
        out_specs=[VMEM] * 2,
        compiler_params=SMALL,
        cost_estimate=cost(1.5),
        name="fuse_two",
    )(*map(in_vmem, (butterfly, fetched, m_high, m_low, after)))


def add_part_kernel(slot, near, coef, high, low, out):
    for b in range(near.shape[0]):
        out[b] = near[b] + apply_split(coef[b], high[b, slot], low[b, slot])


def add_part(slot, *values):
    return pl.pallas_call(
        lambda *refs: add_part_kernel(slot, *refs),
        out_shape=pltpu.VMEM(values[0].shape, F32),
        in_specs=[VMEM] * 4,
        out_specs=VMEM,
        compiler_params=SMALL,
        cost_estimate=cost(0.5),
        name=f"part{slot}",
    )(*map(in_vmem, values))


def level_kernel(own, other, high, low, *rest):
    out = rest[-1]
    for b in range(own.shape[0]):
        out[b] = apply_split(jnp.concatenate([own[b], other[b]], axis=1), high[b], low[b])


def level_step(own, other, high, low, name, *ties):
    values = (own, other, high, low) + ties
    return pl.pallas_call(
        level_kernel,
        out_shape=pltpu.VMEM(own.shape, F32),
        in_specs=[VMEM] * len(values),
        out_specs=VMEM,
        compiler_params=SMALL,
        cost_estimate=cost(0.25),
        name=name,
    )(*map(in_vmem, values))


def last_kernel(two, both, high, low, near, out_hbm, out_buf, sems):
    count = two.shape[0]
    rows = 2 * high.shape[2]
    copies = []
    for b in range(count):
        coef = jnp.concatenate([two[b], both[b]], axis=1)
        weights = (part[b, 2:].reshape(rows, part.shape[-1]) for part in (high, low))
        out_buf[b] = near[b] + apply_split(coef, *weights)
        copies.append(pltpu.make_async_copy(out_buf.at[b], out_hbm.at[b], sems.at[b]))
        copies[b].start()
    for copy in copies:
        copy.wait()


def last_step(*values):
    near = values[-1]
    return pl.pallas_call(
        last_kernel,
        out_shape=jax.ShapeDtypeStruct(near.shape, F32),
        in_specs=[VMEM] * len(values),
        out_specs=ANY,
        scratch_shapes=[
            pltpu.VMEM(near.shape, F32),
            pltpu.SemaphoreType.DMA((near.shape[0],)),
        ],
        compiler_params=SMALL,
        cost_estimate=cost(1.0),
        name="last",
    )(*map(in_vmem, values))


def product(values, weights):
    return jnp.einsum("bri,bio->bro", values, weights, precision=lax.Precision.HIGH)


def stacked(values):
    half = values.shape[-1] // 2
    return jnp.concatenate([values[..., :half], values[..., half:]], axis=1)


def unstacked(values):
    half = values.shape[1] // 2
    return values[:, :half] + turned(values[:, half:])


def exchange(value, mask):
    pairs = [(source, source ^ mask) for source in range(lax.axis_size("box"))]
    return lax.ppermute(value, "box", pairs)


def after(value, other):
    return lax.optimization_barrier((value, other))[0]


def on_device(rhs_block, near_blocks, near_mask, compress, butterfly, expand):
    count = rhs_block.shape[0]
    local_bits = count.bit_length() - 1
    size = lax.axis_size("box")
    even = lax.axis_index("box") % 2 == 0
    masks = near_mask.astype(F32)

    def weights(level, coef):
        return prepare(level, butterfly, coef)

    coef, x = head(rhs_block, compress, butterfly, local_bits)
    first, final = x[:1], x[count - 1 :]
    pairs = [(i, (i - 1 if i % 2 == 0 else i + 1) % size) for i in range(size)]

    other = exchange(coef, 1)
    level2 = weights(2, coef)
    coef = level_step(coef, other, *level2, "level2")

    other = exchange(coef, 2)
    level3 = weights(3, coef)
    inner = exchange(after(jnp.where(even, final, first), level3[0]), 1)
    coef = level_step(coef, other, *level3, "level3")

    other = exchange(coef, 4)
    level4 = weights(4, coef)
    fetched = exchange(after(butterfly[6:7], level4[0]), 32)
    near = product(stacked(after(x, level4[0])), near_blocks[:, 1])
    level5 = weights(5, coef)
    last = fuse_last(butterfly, expand, level4[0])
    coef = level_step(coef, other, *level4, "level4", *level5, *last, near, inner)

    other = exchange(coef, 8)
    fused = fuse_two(butterfly, fetched, *last, coef)
    outer = lax.ppermute(after(jnp.where(even, first, final), coef), "box", pairs)
    coef = level_step(coef, other, *level5, "level5", *fused)

    two = exchange(coef, 32)
    both = exchange(coef, 48)
    one = exchange(coef, 16)
    below = jnp.where(even, outer, inner)
    above = jnp.where(even, inner, outer)
    below, above, _ = lax.optimization_barrier((below, above, coef))
    before = jnp.concatenate([below, x[:-1]], 0) * masks[0][:, None, None]
    behind = jnp.concatenate([x[1:], above], 0) * masks[1][:, None, None]
    near = near + product(stacked(before), near_blocks[:, 0])
    near = unstacked(near + product(stacked(behind), near_blocks[:, 2]))
    near = add_part(0, near, coef, *fused)
    near = add_part(1, near, one, *fused)
    return last_step(two, both, *fused, near)


def solution(mesh):
    placed = (
        P("box", "rhs", None),
        P("box", None, None, None),
        P(None, "box"),
        P("box", None, None),
        P(None, "box", None, None, None),
        P("box", None, None),
    )
    return jax.shard_map(
        on_device, mesh=mesh, in_specs=placed, out_specs=P("box", "rhs", None), check_vma=False
    )
```

```python
import jax
import jax.numpy as jnp
from jax import lax
from jax.experimental import pallas as pl
from jax.experimental.pallas import tpu as pltpu
from jax.sharding import PartitionSpec as P

VMEM = pl.BlockSpec(memory_space=pltpu.VMEM)
ANY = pl.BlockSpec(memory_space=pl.ANY)
SMALL = pltpu.CompilerParams(vmem_limit_bytes=8 << 20)
F32 = jnp.float32
BF16 = jnp.bfloat16


def in_vmem(value):
    return pltpu.with_memory_space_constraint(value, pltpu.VMEM)


def cost(us):
    return pl.CostEstimate(flops=int(us * 1e8), bytes_accessed=int(us * 1e6), transcendentals=0)


def turned(values):
    half = values.shape[-1] // 2
    return jnp.concatenate([-values[..., half:], values[..., :half]], axis=-1)


def split(value):
    high = value.astype(BF16)
    return high, (value - high.astype(F32)).astype(BF16)


def dot(left, right):
    return jnp.dot(left, right, preferred_element_type=F32)


def apply_split(values, high, low):
    rows = values.shape[0]
    first, second = split(values)
    left = jnp.concatenate([first, second], axis=0)
    width = high.shape[1]
    if width > 128:
        both = dot(left, high)
        return both[:rows] + (both[rows:] + dot(first, low))
    both = dot(left, jnp.concatenate([high, low], axis=1))
    return both[:rows, :width] + (both[rows:, :width] + both[:rows, width:])


def complex_dot(values, weights):
    half = values.shape[-1] // 2
    rows = jnp.concatenate([values[:, :half], values[:, half:]], axis=0)
    high, low = split(weights)
    both = apply_split(rows, high, low)
    count = values.shape[0]
    return both[:count] + turned(both[count:])


def level_dot(own, other, weights):
    half = own.shape[-1] // 2
    real = jnp.concatenate([own[:, :half], other[:, :half]], axis=1)
    imag = jnp.concatenate([own[:, half:], other[:, half:]], axis=1)
    high, low = split(weights.reshape(2 * half, weights.shape[-1]))
    count = own.shape[0]
    both = apply_split(jnp.concatenate([real, imag], axis=0), high, low)
    return both[:count] + turned(both[count:])


def head_kernel(x_hbm, c_hbm, w_hbm, out, x_buf, c_buf, w_buf, sems):
    count = x_buf.shape[0]
    copies = []
    for b in range(count):
        copies.append(pltpu.make_async_copy(x_hbm.at[b], x_buf.at[b], sems.at[2 * b]))
        copies.append(pltpu.make_async_copy(c_hbm.at[b], c_buf.at[b], sems.at[2 * b + 1]))
    levels = w_buf.shape[0]
    last = [
        pltpu.make_async_copy(w_hbm.at[level], w_buf.at[level], sems.at[2 * count + level])
        for level in range(levels)
    ]
    for copy in copies + last:
        copy.start()
    coef = []
    for b in range(count):
        copies[2 * b].wait()
        copies[2 * b + 1].wait()
        coef.append(complex_dot(x_buf[b], c_buf[b]))
    for level in range(levels):
        last[level].wait()
        coef = [level_dot(coef[b], coef[b ^ (1 << level)], w_buf[level, b]) for b in range(count)]
    for b in range(count):
        out[b] = coef[b]


def head(x, compress, butterfly, levels):
    count, rows, _ = x.shape
    width = compress.shape[-1]
    return pl.pallas_call(
        head_kernel,
        out_shape=[pltpu.VMEM((count, rows, width), F32), pltpu.VMEM(x.shape, F32)],
        in_specs=[ANY, ANY, ANY],
        out_specs=[VMEM, VMEM],
        scratch_shapes=[
            pltpu.VMEM(compress.shape, F32),
            pltpu.VMEM((levels,) + butterfly.shape[1:], F32),
            pltpu.SemaphoreType.DMA((2 * count + levels,)),
        ],
        cost_estimate=cost(2.5),
        name="head",
    )(x, compress, butterfly)


def prepare_kernel(level, weights_ref, after, high, low):
    del after
    _, count, slots, rank, _ = weights_ref.shape
    for b in range(count):
        for s in range(slots):
            base = 2 * rank * s
            weights = weights_ref[level, b, s]
            high[b, base : base + rank], low[b, base : base + rank] = split(weights)
            base += rank
            high[b, base : base + rank], low[b, base : base + rank] = split(turned(weights))


def prepare(level, butterfly, after):
    _, count, slots, rank, width = butterfly.shape
    shape = pltpu.VMEM((count, 2 * slots * rank, width), BF16)
    return pl.pallas_call(
        lambda *refs: prepare_kernel(level, *refs),
        out_shape=[shape, shape],
        in_specs=[VMEM, VMEM],
        out_specs=[VMEM, VMEM],
        compiler_params=SMALL,
        cost_estimate=cost(0.25),
        name=f"prepare{level}",
    )(in_vmem(butterfly), in_vmem(after))


def store_expanded(high, low, where, weights):
    rank = weights.shape[0]
    high[(*where, slice(0, rank))], low[(*where, slice(0, rank))] = split(weights)
    weights = turned(weights)
    high[(*where, slice(rank, None))], low[(*where, slice(rank, None))] = split(weights)


def fuse_last_kernel(weights_ref, expand_ref, after, high, low):
    del after
    level = weights_ref.shape[0] - 1
    _, count, slots, rank, width = weights_ref.shape
    for b in range(count):
        expand = expand_ref[b]
        expand = jnp.concatenate([expand, turned(expand)], axis=0)
        both = apply_split(weights_ref[level, b].reshape(slots * rank, width), *split(expand))
        for s in range(slots):
            store_expanded(high, low, (b, s), both[s * rank : (s + 1) * rank])


def fuse_last(butterfly, expand, after):
    _, count, slots, rank, width = butterfly.shape
    shape = pltpu.VMEM((count, slots, width, expand.shape[-1]), BF16)
    return pl.pallas_call(
        fuse_last_kernel,
        out_shape=[shape, shape],
        in_specs=[VMEM] * 3,
        out_specs=[VMEM] * 2,
        compiler_params=SMALL,
        cost_estimate=cost(1.0),
        name="fuse_last",
    )(*map(in_vmem, (butterfly, expand, after)))


def fuse_two_kernel(weights_ref, fetched_ref, m_high, m_low, after, high, low):
    del after
    level = weights_ref.shape[0] - 2
    _, count, slots, rank, width = weights_ref.shape
    for b in range(count):
        for half, weights in enumerate((weights_ref[level, b], fetched_ref[0, b])):
            rows = weights.reshape(slots * rank, width)
            both = apply_split(rows, m_high[b, half], m_low[b, half])
            for s in range(slots):
                store_expanded(high, low, (b, 2 * half + s), both[s * rank : (s + 1) * rank])


def fuse_two(butterfly, fetched, m_high, m_low, after):
    count, slots, width, out = m_high.shape
    shape = pltpu.VMEM((count, 2 * slots, width, out), BF16)
    return pl.pallas_call(
        fuse_two_kernel,
        out_shape=[shape, shape],
        in_specs=[VMEM] * 5,
        out_specs=[VMEM] * 2,
        compiler_params=SMALL,
        cost_estimate=cost(1.5),
        name="fuse_two",
    )(*map(in_vmem, (butterfly, fetched, m_high, m_low, after)))


def add_part_kernel(slot, near, coef, high, low, out):
    for b in range(near.shape[0]):
        out[b] = near[b] + apply_split(coef[b], high[b, slot], low[b, slot])


def add_part(slot, *values):
    return pl.pallas_call(
        lambda *refs: add_part_kernel(slot, *refs),
        out_shape=pltpu.VMEM(values[0].shape, F32),
        in_specs=[VMEM] * 4,
        out_specs=VMEM,
        compiler_params=SMALL,
        cost_estimate=cost(0.5),
        name=f"part{slot}",
    )(*map(in_vmem, values))


def level_kernel(own, other, high, low, *rest):
    out = rest[-1]
    for b in range(own.shape[0]):
        out[b] = apply_split(jnp.concatenate([own[b], other[b]], axis=1), high[b], low[b])


def level_step(own, other, high, low, name, *ties):
    values = (own, other, high, low) + ties
    return pl.pallas_call(
        level_kernel,
        out_shape=pltpu.VMEM(own.shape, F32),
        in_specs=[VMEM] * len(values),
        out_specs=VMEM,
        compiler_params=SMALL,
        cost_estimate=cost(0.25),
        name=name,
    )(*map(in_vmem, values))


def last_kernel(two, both, high, low, near, out_hbm, out_buf, sems):
    count = two.shape[0]
    rows = 2 * high.shape[2]
    copies = []
    for b in range(count):
        coef = jnp.concatenate([two[b], both[b]], axis=1)
        weights = (part[b, 2:].reshape(rows, part.shape[-1]) for part in (high, low))
        out_buf[b] = near[b] + apply_split(coef, *weights)
        copies.append(pltpu.make_async_copy(out_buf.at[b], out_hbm.at[b], sems.at[b]))
        copies[b].start()
    for copy in copies:
        copy.wait()


def last_step(*values):
    near = values[-1]
    return pl.pallas_call(
        last_kernel,
        out_shape=jax.ShapeDtypeStruct(near.shape, F32),
        in_specs=[VMEM] * len(values),
        out_specs=ANY,
        scratch_shapes=[
            pltpu.VMEM(near.shape, F32),
            pltpu.SemaphoreType.DMA((near.shape[0],)),
        ],
        compiler_params=SMALL,
        cost_estimate=cost(1.0),
        name="last",
    )(*map(in_vmem, values))


def product(values, weights):
    return jnp.einsum("bri,bio->bro", values, weights, precision=lax.Precision.HIGH)


def stacked(values):
    half = values.shape[-1] // 2
    return jnp.concatenate([values[..., :half], values[..., half:]], axis=1)


def unstacked(values):
    half = values.shape[1] // 2
    return values[:, :half] + turned(values[:, half:])


def exchange(value, mask):
    pairs = [(source, source ^ mask) for source in range(lax.axis_size("box"))]
    return lax.ppermute(value, "box", pairs)


def after(value, other):
    return lax.optimization_barrier((value, other))[0]


def on_device(rhs_block, near_blocks, near_mask, compress, butterfly, expand):
    count = rhs_block.shape[0]
    local_bits = count.bit_length() - 1
    size = lax.axis_size("box")
    even = lax.axis_index("box") % 2 == 0
    masks = near_mask.astype(F32)

    def weights(level, coef):
        return prepare(level, butterfly, coef)

    coef, x = head(rhs_block, compress, butterfly, local_bits)
    first, final = x[:1], x[count - 1 :]
    pairs = [(i, (i - 1 if i % 2 == 0 else i + 1) % size) for i in range(size)]

    other = exchange(coef, 1)
    level2 = weights(2, coef)
    coef = level_step(coef, other, *level2, "level2")

    other = exchange(coef, 2)
    level3 = weights(3, coef)
    inner = exchange(after(jnp.where(even, final, first), level3[0]), 1)
    coef = level_step(coef, other, *level3, "level3")

    other = exchange(coef, 4)
    level4 = weights(4, coef)
    fetched = exchange(after(butterfly[6:7], coef), 32)
    near = product(stacked(after(x, level4[0])), near_blocks[:, 1])
    level5 = weights(5, coef)
    last = fuse_last(butterfly, expand, level4[0])
    coef = level_step(coef, other, *level4, "level4", *level5, *last, near, inner)

    other = exchange(coef, 8)
    fused = fuse_two(butterfly, fetched, *last, coef)
    outer = lax.ppermute(after(jnp.where(even, first, final), coef), "box", pairs)
    coef = level_step(coef, other, *level5, "level5", *fused)

    two = exchange(coef, 32)
    both = exchange(coef, 48)
    one = exchange(coef, 16)
    below = jnp.where(even, outer, inner)
    above = jnp.where(even, inner, outer)
    below, above, _ = lax.optimization_barrier((below, above, coef))
    before = jnp.concatenate([below, x[:-1]], 0) * masks[0][:, None, None]
    behind = jnp.concatenate([x[1:], above], 0) * masks[1][:, None, None]
    near = near + product(stacked(before), near_blocks[:, 0])
    near = unstacked(near + product(stacked(behind), near_blocks[:, 2]))
    near = add_part(0, near, coef, *fused)
    near = add_part(1, near, one, *fused)
    return last_step(two, both, *fused, near)


def solution(mesh):
    placed = (
        P("box", "rhs", None),
        P("box", None, None, None),
        P(None, "box"),
        P("box", None, None),
        P(None, "box", None, None, None),
        P("box", None, None),
    )
    return jax.shard_map(
        on_device, mesh=mesh, in_specs=placed, out_specs=P("box", "rhs", None), check_vma=False
    )
```
